32 devices in a mesh: rows: 8 (over z, y), cols: 4 (over x, core).
Axes of the slice: x: 2, y: 2, z: 4, core: 2. Of those that a mesh axis runs over, the one named last changes fastest.
Arguments:
- trace_limbs: float32 [2, 33554432], P(None, ('cols', 'rows')), parts along dimension 1, may hold values from 0 to 1, as said below
- coset_shift: int32 [1], replicated, may hold values from 1 to 2013265920
Outputs:
- extension: float32 [2, 67108864], P(None, ('cols', 'rows')), parts along dimension 1
The draws below stay inside these ranges and needn't reach their ends.
There are 4 independent parts, one for each index of `cols`. The reference program is written for one: setup_inputs(seed, part) draws one part's arguments, and reference() takes and returns one part's arrays. A program takes and returns all parts, laid end to end along the dimension named above; an argument that names none is the same for every part. Nothing has to cross between parts.
Inputs may be any that keep to these rules, and one draw needn't show every extreme that they name: `trace_limbs`: every entry is a whole multiple of 2**-16, and the entries of the second limb row are below one half.
All inputs are finite; a program needn't handle non-finite values.
Results may differ from the reference program's by a relative error of at most 0.0003.
Values may be sent and summed in bfloat16 or wider, within the bound.
A program may use at most 192 MiB of HBM per device.

```python
import jax
import jax.numpy as jnp

LEN_A = 2048
LEN_B = 4096


def draw_trace_limbs(key, part):
    key = jax.random.fold_in(key, 11)
    low_key, high_key = jax.random.split(key)
    low_part = jax.random.randint(low_key, (LEN_A * LEN_B,), 0, 65536)
    high_part = jax.random.randint(high_key, (LEN_A * LEN_B,), 0, 32768)
    return jnp.stack([low_part, high_part]).astype(jnp.float32) / 65536.0


def setup_inputs(seed: int = 0, part: int = 0) -> dict:
    streams_of = jax.random.split(jax.random.key(seed), 3)
    own_keys = jax.random.split(jax.random.fold_in(streams_of[2], part), 3)
    return {
        "trace_limbs": draw_trace_limbs(jax.random.fold_in(jax.random.fold_in(streams_of[2], part), 71), part),
        "coset_shift": jax.random.randint(streams_of[1], (1,), 1, 2013265921).astype(jnp.int32),
    }


MODULUS = 2013265921


def unity_root(length):
    return pow(pow(31, 15, MODULUS), (1 << 27) // length, MODULUS)


def reduce_product(small_factor, field_factor):
    estimate = jnp.floor(small_factor.astype(jnp.float32) * field_factor.astype(jnp.float32) * (1.0 / MODULUS) + 0.5)
    remainder = small_factor * field_factor - estimate.astype(jnp.int32) * MODULUS
    return jnp.where(remainder < 0, remainder + MODULUS, remainder)


def field_add(first_term, second_term):
    summed = first_term - MODULUS + second_term
    return jnp.where(summed < 0, summed + MODULUS, summed)


def field_sub(first_term, second_term):
    differ = first_term - second_term
    return jnp.where(differ < 0, differ + MODULUS, differ)


def field_mul(factor_one, factor_two):
    high_part = reduce_product(factor_one >> 16, factor_two)
    low_part = reduce_product(factor_one & 65535, factor_two)
    return field_add(reduce_product(jnp.int32(65536), high_part), low_part)


def const_powers(base_value, exponents, bit_count):
    result = jnp.ones_like(exponents)
    for bit_level in range(bit_count):
        factor = jnp.where(((exponents >> bit_level) & 1) == 1, jnp.int32(pow(base_value, 1 << bit_level, MODULUS)), jnp.int32(1))
        result = field_mul(result, factor)
    return result


def traced_powers(base_value, exponents, bit_count):
    result = jnp.ones_like(exponents)
    square = base_value
    for bit_level in range(bit_count):
        result = jnp.where(((exponents >> bit_level) & 1) == 1, field_mul(result, square), result)
        square = field_mul(square, square)
    return result


def power_table(base_value, length):
    low_count = min(64, length)
    low_part = const_powers(base_value, jnp.arange(low_count, dtype=jnp.int32), 6)
    high_count = length // low_count
    high_part = const_powers(pow(base_value, low_count, MODULUS), jnp.arange(high_count, dtype=jnp.int32), max(1, high_count.bit_length()))
    return field_mul(high_part[:, None], low_part[None, :]).reshape(length)


def transform(values, root_table):
    length = values.shape[-1]
    row_count = values.size // length
    state = values.reshape(row_count, length)
    leading = state.T.reshape(1, length * row_count)
    half_span = 1
    while half_span < length and half_span < 128:
        groups = length // (2 * half_span)
        halves = leading.reshape(half_span, 2, groups * row_count)
        even_part = halves[:, 0]
        odd_part = halves[:, 1]
        twiddles = root_table[::groups]
        product = field_mul(odd_part, twiddles[:, None])
        leading = jnp.stack([field_add(even_part, product), field_sub(even_part, product)], 0).reshape(2 * half_span, groups * row_count)
        half_span = half_span * 2
    state = leading.reshape(half_span, length // half_span, row_count).transpose(2, 1, 0).reshape(row_count, length)
    while half_span < length:
        groups = length // (2 * half_span)
        halves = state.reshape(row_count, 2, length // 2)
        even_part = halves[:, 0]
        odd_part = halves[:, 1]
        twiddles = jnp.tile(root_table[::groups], groups)
        product = field_mul(odd_part, twiddles[None, :])
        sum_part = field_add(even_part, product).reshape(row_count, groups, half_span)
        diff_part = field_sub(even_part, product).reshape(row_count, groups, half_span)
        state = jnp.stack([sum_part, diff_part], 2).reshape(row_count, length)
        half_span = half_span * 2
    return state.reshape(values.shape)


def from_limbs(trace_limbs):
    low_part = (trace_limbs[0] * 65536.0).astype(jnp.int32)
    high_part = (trace_limbs[1] * 65536.0).astype(jnp.int32)
    joined = high_part * 65536 + low_part
    return jnp.where(joined >= MODULUS, joined - MODULUS, joined)


def to_limbs(field_values):
    return jnp.stack([(field_values & 65535).astype(jnp.float32), (field_values >> 16).astype(jnp.float32)]) / 65536.0


def reference(trace_limbs, coset_shift):
    values = from_limbs(trace_limbs)
    trace_len = values.shape[0]
    back_root = pow(unity_root(trace_len), MODULUS - 2, MODULUS)
    coeffs = transform(values, power_table(back_root, trace_len // 2))
    inverse_len = pow(trace_len, MODULUS - 2, MODULUS)
    shift_base = coset_shift[0]
    low_powers = field_mul(traced_powers(shift_base, jnp.arange(64, dtype=jnp.int32), 6), jnp.int32(inverse_len))
    step_power = traced_powers(shift_base, jnp.array([64], dtype=jnp.int32), 7)[0]
    high_count = trace_len // 64
    high_powers = traced_powers(step_power, jnp.arange(high_count, dtype=jnp.int32), high_count.bit_length())
    weights = field_mul(high_powers[:, None], low_powers[None, :]).reshape(trace_len)
    shifted = jnp.concatenate([field_mul(coeffs, weights), jnp.zeros((trace_len,), jnp.int32)])
    extended = transform(shifted, power_table(unity_root(2 * trace_len), trace_len))
    return to_limbs(extended)
```

```python
import functools

import jax
import jax.numpy as jnp
import numpy as np
from jax import lax
from jax.experimental import pallas as pl
from jax.experimental.pallas import tpu as pltpu
from jax.sharding import PartitionSpec as P

MODULUS = 2013265921
LOG_TRACE = 23
TRACE_LEN = 1 << LOG_TRACE
VMEM_BYTES = 56 * 1024 * 1024


def unity_root(length):
    return pow(pow(31, 15, MODULUS), (1 << 27) // length, MODULUS)


def inverse_of(value):
    return pow(value, MODULUS - 2, MODULUS)


def np_powers(base, count):
    table = np.ones(1, np.uint64)
    step = base
    while table.size < count:
        table = np.concatenate([table, table * np.uint64(step) % np.uint64(MODULUS)])
        step = step * step % MODULUS
    return table[:count].astype(np.int64)


def centred(values):
    return np.where(values > MODULUS // 2, values - MODULUS, values)


def np_pair(values):
    values = np.asarray(values, np.int64) % MODULUS
    lifted = values * 65536 % MODULUS
    return centred(values).astype(np.int32), centred(lifted).astype(np.int32)


def np_digits(values):
    digits = []
    rest = centred(np.asarray(values, np.int64) % MODULUS)
    for _ in range(3):
        above = (rest + 128) >> 8
        digits.append(rest - (above << 8))
        rest = above
    return digits + [rest]


def np_left_matrix(base):
    lifted = [base * (1 << (8 * a)) % MODULUS for a in range(4)]
    wide = np.concatenate(lifted, 1)
    return np.concatenate(np_digits(wide), 0).astype(jnp.bfloat16)


def np_right_matrix(base):
    lifted = [base * (1 << (8 * a)) % MODULUS for a in range(4)]
    tall = np.concatenate(lifted, 0)
    return np.concatenate(np_digits(tall), 1).astype(jnp.bfloat16)


def outer_powers(root, rows, columns, order):
    table = np_powers(root, order)
    exponents = np.arange(rows)[:, None] * np.arange(columns)[None, :]
    return table[exponents % order]


def times(x, plain, lifted):
    high = x >> 16
    low = x & 65535
    scale = jnp.float32(1.0 / MODULUS)
    estimate = high.astype(jnp.float32) * (lifted.astype(jnp.float32) * scale) + low.astype(
        jnp.float32
    ) * (plain.astype(jnp.float32) * scale)
    quotient = jnp.floor(estimate + 0.5).astype(jnp.int32)
    return high * lifted + low * plain - quotient * jnp.int32(MODULUS)


def times_const(x, value):
    plain, lifted = np_pair(np.int64(value))
    return times(x, jnp.int32(int(plain)), jnp.int32(int(lifted)))


def lift(x):
    return times_const(x, 65536)


def split_digits(x):
    digits = []
    for _ in range(3):
        above = (x + 128) >> 8
        digits.append((x - (above << 8)).astype(jnp.float32).astype(jnp.bfloat16))
        x = above
    return digits + [x.astype(jnp.float32).astype(jnp.bfloat16)]


def join_sums(sums):
    scale = 1.0 / MODULUS
    estimate = sums[0] * jnp.float32(scale)
    total = sums[0].astype(jnp.int32)
    for place in range(1, 4):
        estimate = estimate + sums[place] * jnp.float32(scale * (1 << (8 * place)))
        total = total + (sums[place].astype(jnp.int32) << (8 * place))
    quotient = jnp.floor(estimate + 0.5).astype(jnp.int32)
    return total - quotient * jnp.int32(MODULUS)


def dft_left(matrix, x):
    digits = jnp.concatenate(split_digits(x), 0)
    sums = jnp.dot(matrix, digits, preferred_element_type=jnp.float32)
    rows = sums.shape[0] // 4
    return join_sums([sums[i * rows : (i + 1) * rows] for i in range(4)])


def dft_right(x, matrix):
    digits = jnp.concatenate(split_digits(x), 1)
    sums = jnp.dot(digits, matrix, preferred_element_type=jnp.float32)
    columns = sums.shape[1] // 4
    return join_sums([sums[:, i * columns : (i + 1) * columns] for i in range(4)])


def canonical(x):
    return jnp.where(x < 0, x + MODULUS, x)


def traced_left_matrix(base):
    lifted = [base] + [times_const(base, 1 << (8 * a)) for a in range(1, 4)]
    return jnp.concatenate(split_digits(jnp.concatenate(lifted, 1)), 0)


def shift_powers(shift):
    squares = [shift]
    for _ in range(LOG_TRACE - 1):
        squares.append(times(squares[-1], squares[-1], lift(squares[-1])))
    index = jnp.arange(256, dtype=jnp.int32)
    vectors = []
    for group in range(3):
        result = jnp.ones((256,), jnp.int32)
        for bit in range(min(8, LOG_TRACE - 8 * group)):
            square = squares[8 * group + bit]
            taken = times(result, square, lift(square))
            result = jnp.where((index >> bit) & 1 == 1, taken, result)
        vectors.append(result)
    return vectors[0], vectors[1], vectors[2][:128]


def first_kernel(x_ref, matrix_ref, plain_ref, lifted_ref, out_ref):
    y = dft_left(matrix_ref[...], x_ref[...])
    out_ref[...] = times(y, plain_ref[...], lifted_ref[...])


def last_kernel(x_ref, matrix_ref, plain_ref, lifted_ref, out_ref):
    x = times(x_ref[...], plain_ref[...], lifted_ref[...])
    out_ref[...] = canonical(dft_left(matrix_ref[...], x))


def line_pass(body, x, matrix, plain, lifted, width):
    rows, columns = x.shape
    block = pl.BlockSpec((rows, width), lambda i: (0, i))
    return pl.pallas_call(
        body,
        grid=(columns // width,),
        in_specs=[block, pl.BlockSpec(matrix.shape, lambda i: (0, 0)), block, block],
        out_specs=block,
        out_shape=jax.ShapeDtypeStruct(x.shape, jnp.int32),
        compiler_params=pltpu.CompilerParams(vmem_limit_bytes=VMEM_BYTES),
    )(x, matrix, plain, lifted)


def middle_kernel(group, x_ref, m2, p2, l2, m3, pw, lw, m4, p4, l4, m5, out_ref):
    lines = [x_ref[g] for g in range(group)]
    z = dft_left(m2[...], jnp.concatenate(lines, 1))
    lines = [times(z[:, g * 128 : (g + 1) * 128], p2[...], l2[...]) for g in range(group)]
    c = dft_right(jnp.concatenate(lines, 0), m3[...])
    lines = [times(c[g * 256 : (g + 1) * 256], pw[...], lw[...]) for g in range(group)]
    y = dft_right(jnp.concatenate(lines, 0), m4[...])
    lines = [times(y[g * 256 : (g + 1) * 256], p4[...], l4[...]) for g in range(group)]
    v = dft_left(m5[...], jnp.concatenate(lines, 1))
    for g in range(group):
        out_ref[g] = v[:, g * 256 : (g + 1) * 256]


def middle_pass(x, tables, group):
    count = x.shape[0]
    whole = [pl.BlockSpec(t.shape, lambda i: (0, 0)) for t in tables]
    return pl.pallas_call(
        functools.partial(middle_kernel, group),
        grid=(count // group,),
        in_specs=[pl.BlockSpec((group, 256, 128), lambda i: (i, 0, 0))] + whole,
        out_specs=pl.BlockSpec((group, 256, 256), lambda i: (i, 0, 0)),
        out_shape=jax.ShapeDtypeStruct((count, 256, 256), jnp.int32),
        compiler_params=pltpu.CompilerParams(vmem_limit_bytes=VMEM_BYTES),
    )(x, *tables)


def from_limbs(trace_limbs):
    low_part = (trace_limbs[0] * 65536.0).astype(jnp.int32)
    high_part = (trace_limbs[1] * 65536.0).astype(jnp.int32)
    joined = high_part * 65536 + low_part
    return jnp.where(joined >= MODULUS, joined - MODULUS, joined)


def to_limbs(field_values):
    return (
        jnp.stack(
            [(field_values & 65535).astype(jnp.float32), (field_values >> 16).astype(jnp.float32)]
        )
        / 65536.0
    )


def exchange(x):
    return lax.all_to_all(x, "rows", split_axis=0, concat_axis=0, tiled=True)


def on_device(trace_limbs, coset_shift):
    devices = lax.axis_size("rows")
    position = lax.axis_index("rows")
    per = 256 // devices
    chunk = 32768 // devices
    ext_len = 2 * TRACE_LEN
    back = inverse_of(unity_root(TRACE_LEN))
    back_256 = inverse_of(unity_root(256))
    ahead = unity_root(ext_len)

    p1, l1 = np_pair(outer_powers(back, 256, chunk, TRACE_LEN))
    p6, l6 = np_pair(outer_powers(ahead, 256, 2 * chunk, ext_len))
    step1 = np_powers(pow(back, chunk, MODULUS), 256 * devices)
    step6 = np_powers(pow(ahead, 2 * chunk, MODULUS), 256 * devices)
    exponents = np.arange(devices)[:, None] * np.arange(256)[None, :] % (256 * devices)
    row1 = np.stack(np_pair(step1[exponents]))
    row6 = np.stack(np_pair(step6[exponents]))
    dft_back = outer_powers(back_256, 256, 256, 256)
    dft_ahead = outer_powers(unity_root(256), 256, 256, 256)

    row1 = lax.dynamic_index_in_dim(jnp.asarray(row1), position, 1, False)
    m1 = traced_left_matrix(
        times(jnp.asarray(np_pair(dft_back)[0]), row1[0][:, None], row1[1][:, None])
    )
    s1, s2, s3 = shift_powers(coset_shift[0])
    s3 = times_const(s3, inverse_of(TRACE_LEN))
    pw = times(s2[:, None], s3[None, :], lift(s3)[None, :])
    lw = lift(pw)
    row6 = lax.dynamic_index_in_dim(jnp.asarray(row6), position, 1, False)
    row6 = times(s1, row6[0], row6[1])
    m6 = traced_left_matrix(
        times(jnp.asarray(np_pair(dft_ahead)[0]), row6[None, :], lift(row6)[None, :])
    )

    p2, l2 = np_pair(outer_powers(inverse_of(unity_root(32768)), 256, 128, 32768))
    p4, l4 = np_pair(outer_powers(unity_root(65536), 256, 256, 65536))
    m2 = np_left_matrix(dft_back)
    m3 = np_right_matrix(outer_powers(inverse_of(unity_root(128)), 128, 128, 128))
    m4 = np_right_matrix(dft_ahead[:128])
    m5 = np_left_matrix(dft_ahead)

    values = from_limbs(trace_limbs)
    x = values.reshape(per, devices, chunk).transpose(1, 0, 2)
    x = exchange(x).reshape(256, chunk)
    x = line_pass(first_kernel, x, m1, jnp.asarray(p1), jnp.asarray(l1), min(512, chunk))
    x = exchange(x.reshape(devices, per, chunk))
    x = x.reshape(devices, per, per, 128).transpose(1, 0, 2, 3).reshape(per, 256, 128)
    tables = [m2, p2, l2, m3, pw, lw, m4, p4, l4, m5]
    x = middle_pass(x, [jnp.asarray(t) for t in tables], 2)
    x = x.reshape(per, devices, per, 256).transpose(1, 0, 2, 3)
    x = exchange(x).reshape(256, 2 * chunk)
    x = line_pass(last_kernel, x, m6, jnp.asarray(p6), jnp.asarray(l6), min(512, 2 * chunk))
    x = exchange(x.reshape(devices, per, 2 * chunk))
    x = x.transpose(1, 0, 2).reshape(per * devices * 2 * chunk)
    return to_limbs(x)


def solution(mesh):
    placed = (P(None, ("cols", "rows")), P())
    return jax.shard_map(
        on_device, mesh=mesh, in_specs=placed, out_specs=P(None, ("cols", "rows")), check_vma=False
    )
```
